1024 devices in a mesh: island: 16 (over z_lo, core), dev: 64 (over x, y, z_hi).
Axes of the slice: x: 4, y: 8, z: 16 (z_hi: 2, z_lo: 8; z = z_hi * 8 + z_lo), core: 2. Of those that a mesh axis runs over, the one named last changes fastest.
Arguments:
- image_embed: bfloat16 [262144, 1152], P(('island', 'dev')), may hold values from -6 to 6
- text_feat: bfloat16 [262144, 1152], P(('island', 'dev')), may hold values from -1.1953125 to 1.1953125
- text_proj: bfloat16 [1152, 1152], P('dev'), may hold values from -0.1875 to 0.1875
- log_scale: float32 [], replicated, may hold values from 1.5 to 2.3
- bias: float32 [], replicated, may hold values from -3 to -1
Outputs:
- grad_text: bfloat16 [262144, 1152], P(('island', 'dev'))
The draws below stay inside these ranges and needn't reach their ends.
All inputs are finite; a program needn't handle non-finite values.
Results may differ from the reference program's by a relative error of at most 0.0065.
Values may be sent and summed in bfloat16 or wider, within the bound.
No kernel may reach another device: no remote copies, remote signals or barrier semaphores. Data moves between devices by JAX's collectives and lax.ppermute only.
A program may use at most 32 MiB of HBM per device.

```python
import jax
import jax.numpy as jnp
from jax import lax

D = 1152
ROWS = 256
BATCH = 262144
N_ISLAND = 16
N_DEV = 64


def level_of(own_key, shape, pieces, smallest, top_value):
    loudness = 1.0
    for position, parts in pieces:
        steps = jax.random.uniform(jax.random.fold_in(jax.random.fold_in(own_key, 6), position), (parts,), jnp.float32, smallest / len(pieces), top_value / len(pieces))
        loudness = loudness * jnp.repeat(jnp.exp(steps), shape[position] // parts).reshape((-1,) + (1,) * (len(shape) - 1 - position))
    return loudness


def centred(rng, extent, spread, bound, split=(), held_as=jnp.bfloat16):
    loudness = level_of(rng, extent, split, -0.22, 0.18) if split else 1.0
    result = jax.random.normal(rng, extent, jnp.float32) * spread * loudness
    return jnp.minimum(jnp.maximum(result, -bound), bound).astype(held_as)


def setup_inputs(seed: int = 0) -> dict:
    key_of = jax.random.split(jax.random.key(seed), 6)
    image_embed = centred(key_of[0], (BATCH, D), 1.0, 6.0, ((0, 1024),))
    text_feat = centred(key_of[1], (BATCH, D), 0.2, 1.1953125, ((0, 1024),))
    text_proj = centred(key_of[2], (D, D), D ** -0.5, 0.1875, ((0, 64),))
    log_scale = jnp.clip(jax.random.uniform(key_of[3], (), jnp.float32, 1.5, 2.3), 1.5, 2.3)
    bias = jnp.clip(jax.random.uniform(key_of[4], (), jnp.float32, -3.0, -1.0), -3.0, -1.0)
    return {"image_embed": image_embed, "text_feat": text_feat, "text_proj": text_proj, "log_scale": log_scale, "bias": bias}


norm_eps = 1e-06

def reference(image_embed, text_feat, text_proj, log_scale, bias):
    image_f = image_embed.astype(jnp.float32)
    unit_img = (image_f * lax.rsqrt(lax.optimization_barrier(jnp.sum(image_f * image_f, axis=1, keepdims=True)) + norm_eps)).astype(jnp.bfloat16)
    hidden = jnp.dot(text_feat, text_proj, preferred_element_type=jnp.float32)
    inv_norm = lax.rsqrt(lax.optimization_barrier(jnp.sum(hidden * hidden, axis=1, keepdims=True)) + norm_eps)
    unit_txt = hidden * inv_norm
    text_b = unit_txt.astype(jnp.bfloat16)
    logit_scale = jnp.exp(log_scale)
    feat_width = text_b.shape[1]
    text_grid = text_b.reshape(N_ISLAND, N_DEV, ROWS, feat_width)
    image_grid = unit_img.reshape(N_ISLAND, N_DEV, ROWS, feat_width)
    matched = jnp.eye(ROWS, dtype=jnp.float32)
    turn_count = min(4, N_ISLAND)

    def one_island(island):
        texts = lax.dynamic_index_in_dim(text_grid, island, 0, keepdims=False).astype(jnp.float32)
        total = jnp.zeros((N_DEV, ROWS, feat_width), jnp.float32)
        for turn in range(turn_count):
            other = ((island + turn) % N_ISLAND).astype(jnp.int32)
            images = lax.dynamic_index_in_dim(image_grid, other, 0, keepdims=False).astype(jnp.float32)
            scores = logit_scale * jnp.einsum('drk,dsk->drs', texts, images) + bias
            opening = matched if turn == 0 else jnp.zeros_like(matched)
            weights = (jax.nn.sigmoid(scores) - opening[None]).astype(jnp.bfloat16)
            total = total + logit_scale * jnp.einsum('drs,dsk->drk', weights.astype(jnp.float32), images)
        return total
    grad_unit = lax.map(one_island, jnp.arange(N_ISLAND, dtype=jnp.int32)).reshape(-1, feat_width)
    radial = lax.optimization_barrier(jnp.sum(unit_txt * grad_unit, axis=1, keepdims=True))
    grad_hidden = ((grad_unit - unit_txt * radial) * inv_norm).astype(jnp.bfloat16)
    grad_text = jnp.dot(grad_hidden, text_proj.T, preferred_element_type=jnp.float32)
    return grad_text.astype(jnp.bfloat16)
```

```python
import jax
import jax.numpy as jnp
from jax import lax
from jax.experimental import pallas as pl
from jax.experimental.pallas import tpu as pltpu
from jax.sharding import PartitionSpec as P

norm_eps = 1e-06
AXES = ("island", "dev")
NX, NY, NZH = 4, 8, 2


def coords(i, n_dev):
    isl, dev = divmod(i, n_dev)
    return isl, dev // (NY * NZH), dev // NZH % NY, dev % NZH


def moved(value, to):
    n_isl, n_dev = lax.axis_size("island"), lax.axis_size("dev")
    pairs = []
    for i in range(n_isl * n_dev):
        target = to(*coords(i, n_dev))
        if target is not None:
            isl, x, y, zh = target
            pairs.append(
                (i, (isl % n_isl) * n_dev + ((x % NX) * NY + y % NY) * NZH + zh % NZH)
            )
    return lax.ppermute(value, AXES, pairs)


def tail_kernel(
    idx, scal, im0, im1, im2, im3, text,
    m0, mm, m2, mp, o0, om, o2, op,
    out_ref,
    raw, unit, txt, sets, full, hid, sems,
):
    x, y, c = idx[0], idx[1], idx[2]
    rows = out_ref.shape[0]
    copies = []
    for k, src in enumerate((im0, im1, im2, im3)):
        copies.append(pltpu.make_async_copy(src, raw.at[pl.ds(k * rows, rows)], sems.at[k]))
    copies.append(pltpu.make_async_copy(text, txt, sems.at[4]))
    k = 5
    for core, group in ((c, (m0, mp, m2, mm)), (1 - c, (o0, op, o2, om))):
        for rel, src in enumerate(group):
            slot = core * NX + lax.rem(x + rel, NX)
            copies.append(pltpu.make_async_copy(src, sets.at[slot], sems.at[k]))
            k += 1
    for copy in copies:
        copy.start()

    for k in range(4):
        copies[k].wait()
        f = raw[pl.ds(k * rows, rows), :].astype(jnp.float32)
        s = lax.rsqrt(jnp.sum(f * f, axis=1, keepdims=True) + norm_eps)
        unit[pl.ds(k * rows, rows), :] = (f * s).astype(jnp.bfloat16)

    for copy in copies[4:]:
        copy.wait()

    for xx in range(NX):
        for half in range(2):
            slabs = []
            for yy in range(half * 4, half * 4 + 4):
                j = lax.rem(y - yy + NY, NY)
                far = (j >= 4).astype(jnp.int32)
                pos = jnp.where(j < 4, j, 7 - j)
                slabs.append(sets[far * NX + xx, pos].astype(jnp.float32))
            block = jnp.concatenate(slabs, axis=0).astype(jnp.bfloat16)
            full[pl.ds(xx * 288 + half * 144, 144), :] = block

    hidden = jnp.dot(txt[...], full[...], preferred_element_type=jnp.float32)
    inv = lax.rsqrt(jnp.sum(hidden * hidden, axis=1, keepdims=True) + norm_eps)
    hid[...] = hidden * inv
    text_b = hid[...].astype(jnp.bfloat16)
    scale, bias = scal[0], scal[1]
    grad = jnp.zeros(hid.shape, jnp.float32)
    for t in range(4):
        u = unit[pl.ds(t * rows, rows), :]
        scores = scale * lax.dot_general(
            text_b, u, (((1,), (1,)), ((), ())), preferred_element_type=jnp.float32
        ) + bias
        probs = jax.nn.sigmoid(scores)
        if t == 0:
            r = lax.broadcasted_iota(jnp.int32, (rows, rows), 0)
            s = lax.broadcasted_iota(jnp.int32, (rows, rows), 1)
            probs = probs - (r == s).astype(jnp.float32)
        grad = grad + jnp.dot(
            probs.astype(jnp.bfloat16), u, preferred_element_type=jnp.float32
        )
    grad = grad * scale
    unit_txt = hid[...]
    radial = jnp.sum(unit_txt * grad, axis=1, keepdims=True)
    grad_hidden = ((grad - unit_txt * radial) * inv).astype(jnp.bfloat16)
    out_ref[...] = lax.dot_general(
        grad_hidden, full[...], (((1,), (1,)), ((), ())), preferred_element_type=jnp.float32
    ).astype(jnp.bfloat16)


def body(image_embed, text_feat, text_proj, log_scale, bias):
    rows, width = text_feat.shape
    isl = lax.axis_index("island").astype(jnp.int32)
    dev = lax.axis_index("dev").astype(jnp.int32)
    c, x, y, zh = isl % 2, dev // (NY * NZH), dev // NZH % NY, dev % NZH

    far = moved(text_proj, lambda i, x, y, z: (i, x, y - i % 2, 1 - z))
    near = moved(text_proj, lambda i, x, y, z: (i, x, y - 1, z) if i % 2 else None)
    base = jnp.where(c == 0, text_proj, near)
    pair = jnp.where(
        zh == 0, jnp.concatenate([base, far]), jnp.concatenate([far, base])
    )

    two = moved(image_embed, lambda i, x, y, z: (i - 2, x, y, z))
    chip = moved(image_embed, lambda i, x, y, z: (i ^ 1, x, y, z))

    got = [
        moved(pair, lambda i, x, y, z, k=k: (i, x, y + (-k if i % 2 else k), z))
        for k in (1, 2, 3)
    ]
    mine = jnp.stack([pair] + got)
    minus = moved(mine, lambda i, x, y, z: (i, x + 1, y, z))
    plus = moved(mine, lambda i, x, y, z: (i, x - 1, y, z))
    o0 = moved(mine, lambda i, x, y, z: (i ^ 1, x, y, z))
    swapped = moved(two, lambda i, x, y, z: (i ^ 1, x, y, z))
    ahead = moved(two, lambda i, x, y, z: (i - 1, x, y, z) if i % 2 == 0 else None)

    across = moved(
        jnp.where(c == 0, minus, plus), lambda i, x, y, z: (i, x + (-1 if i % 2 else 1), y, z)
    )
    om = moved(minus, lambda i, x, y, z: (i ^ 1, x, y, z))
    op = moved(plus, lambda i, x, y, z: (i ^ 1, x, y, z))
    o2 = moved(across, lambda i, x, y, z: (i ^ 1, x, y, z))

    im1 = jnp.where(c == 0, chip, ahead)
    idx = jnp.stack([x, y, c])
    scal = jnp.stack([jnp.exp(log_scale), bias])
    any_spec = pl.BlockSpec(memory_space=pl.ANY)
    smem = pl.BlockSpec(memory_space=pltpu.SMEM)
    return pl.pallas_call(
        tail_kernel,
        out_shape=jax.ShapeDtypeStruct((rows, width), jnp.bfloat16),
        in_specs=[smem, smem] + [any_spec] * 13,
        out_specs=pl.BlockSpec(memory_space=pltpu.VMEM),
        scratch_shapes=[
            pltpu.VMEM((4 * rows, width), jnp.bfloat16),
            pltpu.VMEM((4 * rows, width), jnp.bfloat16),
            pltpu.VMEM((rows, width), jnp.bfloat16),
            pltpu.VMEM((2 * NX, 4, 36, width), jnp.bfloat16),
            pltpu.VMEM((width, width), jnp.bfloat16),
            pltpu.VMEM((rows, width), jnp.float32),
            pltpu.SemaphoreType.DMA((13,)),
        ],
        compiler_params=pltpu.CompilerParams(vmem_limit_bytes=48 * 1024 * 1024),
        cost_estimate=pl.CostEstimate(
            flops=2 * 2 * rows * width * (width + 4 * rows),
            bytes_accessed=8 * 1024 * 1024,
            transcendentals=4 * rows * rows,
        ),
    )(
        idx, scal, image_embed, im1, two, swapped, text_feat,
        mine, minus, across, plus, o0, om, o2, op,
    )


def solution(mesh):
    placed = (P(AXES, None), P(AXES, None), P("dev", None), P(), P())
    return jax.shard_map(
        body, mesh=mesh, in_specs=placed, out_specs=P(AXES, None), check_vma=False
    )
```

```python
import jax
import jax.numpy as jnp
from jax import lax
from jax.experimental import pallas as pl
from jax.experimental.pallas import tpu as pltpu
from jax.sharding import PartitionSpec as P

norm_eps = 1e-06
AXES = ("island", "dev")
NX, NY, NZH = 4, 8, 2


def coords(i, n_dev):
    isl, dev = divmod(i, n_dev)
    return isl, dev // (NY * NZH), dev // NZH % NY, dev % NZH


def moved(value, to):
    n_isl, n_dev = lax.axis_size("island"), lax.axis_size("dev")
    pairs = []
    for i in range(n_isl * n_dev):
        target = to(*coords(i, n_dev))
        if target is not None:
            isl, x, y, zh = target
            pairs.append(
                (i, (isl % n_isl) * n_dev + ((x % NX) * NY + y % NY) * NZH + zh % NZH)
            )
    return lax.ppermute(value, AXES, pairs)


def place():
    isl = lax.axis_index("island").astype(jnp.int32)
    dev = lax.axis_index("dev").astype(jnp.int32)
    return dev >> 4, (dev >> 1) & 7, dev & 1, isl & 1, isl


def ordered(y, c, mine, other, out, at):
    for half in range(2):
        slabs = []
        for yy in range(half * 4, half * 4 + 4):
            j = (y - yy) & 7
            far = (j >= 4).astype(jnp.int32)
            pos = jnp.where(j < 4, j, 7 - j)
            slab = jnp.where(far == c, mine[pos], other[pos])
            slabs.append(slab.astype(jnp.float32))
        block = jnp.concatenate(slabs, axis=0).astype(jnp.bfloat16)
        out[pl.ds(at + half * 144, 144), :] = block


def column_kernel(mine, other, out):
    _, y, _, c, _ = place()
    ordered(y, c, mine, other, out, 0)


def column(mine, other):
    width = mine.shape[-1]
    return pl.pallas_call(
        column_kernel,
        out_shape=jax.ShapeDtypeStruct((NY * 36, width), jnp.bfloat16),
        cost_estimate=pl.CostEstimate(
            flops=NY * 36 * width, bytes_accessed=4 * NY * 36 * width, transcendentals=0
        ),
    )(mine, other)


def unit_kernel(im0, im1, wrap, im2, im3, out, raw, sems):
    rows = im0.shape[0]
    last = place()[4] == lax.axis_size("island") - 1
    copies = [
        pltpu.make_async_copy(src, raw.at[k], sems.at[k])
        for k, src in enumerate((im0, im1, im2, im3))
    ]
    for k in (0, 2, 3):
        copies[k].start()

    @pl.when(last)
    def _():
        pltpu.make_async_copy(wrap, raw.at[1], sems.at[1]).start()

    @pl.when(jnp.logical_not(last))
    def _():
        copies[1].start()

    for k in (0, 2, 3, 1):
        copies[k].wait()
        f = raw[k].astype(jnp.float32)
        s = lax.rsqrt(jnp.sum(f * f, axis=1, keepdims=True) + norm_eps)
        out[pl.ds(k * rows, rows), :] = (f * s).astype(jnp.bfloat16)


def tail_kernel(scal, unit, text, col, xcol, ocol, mcol, out_ref, full, hid, sems):
    x, _, _, c, _ = place()
    rows = out_ref.shape[0]
    step = jnp.where(c == 0, NX - 1, 1)
    wheres = (x, (x + step) & 3, (x + NX - step) & 3, (x + 2) & 3)
    copies = [
        pltpu.make_async_copy(src, full.at[pl.ds(pl.multiple_of(at * 288, 288), 288)], sems.at[k])
        for k, (src, at) in enumerate(zip((col, xcol, ocol, mcol), wheres))
    ]
    for copy in copies:
        copy.start()
    for copy in copies:
        copy.wait()
    hidden = jnp.dot(text[...], full[...], preferred_element_type=jnp.float32)
    inv = lax.rsqrt(jnp.sum(hidden * hidden, axis=1, keepdims=True) + norm_eps)
    hid[...] = hidden * inv
    text_b = hid[...].astype(jnp.bfloat16)
    scale, bias = scal[0], scal[1]
    scores = scale * lax.dot_general(
        text_b, unit[...], (((1,), (1,)), ((), ())), preferred_element_type=jnp.float32
    ) + bias
    r = lax.broadcasted_iota(jnp.int32, scores.shape, 0)
    s = lax.broadcasted_iota(jnp.int32, scores.shape, 1)
    probs = jax.nn.sigmoid(scores) - (r == s).astype(jnp.float32)
    grad = scale * jnp.dot(
        probs.astype(jnp.bfloat16), unit[...], preferred_element_type=jnp.float32
    )
    unit_txt = hid[...]
    radial = jnp.sum(unit_txt * grad, axis=1, keepdims=True)
    grad_hidden = ((grad - unit_txt * radial) * inv).astype(jnp.bfloat16)
    out_ref[...] = lax.dot_general(
        grad_hidden, full[...], (((1,), (1,)), ((), ())), preferred_element_type=jnp.float32
    ).astype(jnp.bfloat16)


def body(image_embed, text_feat, text_proj, log_scale, bias):
    rows, width = text_feat.shape
    x, y, zh, c, isl = place()
    n_isl = lax.axis_size("island")
    vmem = pl.BlockSpec(memory_space=pltpu.VMEM)
    smem = pl.BlockSpec(memory_space=pltpu.SMEM)
    anyw = pl.BlockSpec(memory_space=pl.ANY)

    far = moved(text_proj, lambda i, x, y, z: (i ^ 8, x, y - i % 2, 1 - z))
    near = moved(text_proj, lambda i, x, y, z: (i, x, y - 1, z) if i % 2 else None)
    base = jnp.where(c == 0, text_proj, near)
    pair = jnp.where(
        zh == 0, jnp.concatenate([base, far]), jnp.concatenate([far, base])
    )

    wrap2 = moved(image_embed, lambda i, x, y, z: (i - 2, x, y, z) if i < 2 else None)
    wrap3 = moved(image_embed, lambda i, x, y, z: (i - 3, x, y, z) if i == 2 else None)
    wrap2, wrap3 = lax.optimization_barrier((wrap2, wrap3))
    held = lax.optimization_barrier((image_embed, far))[0]
    near2 = moved(held, lambda i, x, y, z: (i - 2, x, y, z) if i >= 2 else None)
    two = jnp.where(isl >= n_isl - 2, wrap2, near2)

    got = [
        moved(pair, lambda i, x, y, z, k=k: (i, x, y + (-k if i % 2 else k), z))
        for k in (1, 2, 3)
    ]
    mine = jnp.stack([pair] + got)
    mid = moved(mine, lambda i, x, y, z: (i, x + 2, y, z))
    other = moved(mine, lambda i, x, y, z: (i ^ 1, x, y, z))
    col = column(mine, other)
    xcol = moved(col, lambda i, x, y, z: (i, x + (-1 if i % 2 else 1), y, z))
    two_ = lax.optimization_barrier((two, col))[0]
    one = moved(
        jnp.where(c == 0, two_, image_embed),
        lambda i, x, y, z: (i - 1, x, y, z) if i > 0 else None,
    )
    swapped = moved(two_, lambda i, x, y, z: (i ^ 1, x, y, z))
    mid_ = lax.optimization_barrier((mid, swapped))[0]
    omid = moved(mid_, lambda i, x, y, z: (i ^ 1, x, y, z))
    mcol = column(mid, omid)
    xcol_ = lax.optimization_barrier((xcol, mcol, one))[0]
    ocol = moved(xcol_, lambda i, x, y, z: (i ^ 1, x, y, z))

    unit = pl.pallas_call(
        unit_kernel,
        out_shape=jax.ShapeDtypeStruct((4 * rows, width), jnp.bfloat16),
        in_specs=[anyw] * 5,
        out_specs=vmem,
        scratch_shapes=[
            pltpu.VMEM((4, rows, width), jnp.bfloat16),
            pltpu.SemaphoreType.DMA((4,)),
        ],
        compiler_params=pltpu.CompilerParams(vmem_limit_bytes=16 * 1024 * 1024),
        cost_estimate=pl.CostEstimate(
            flops=12 * rows * width, bytes_accessed=16 * rows * width, transcendentals=4 * rows
        ),
    )(image_embed, one, wrap3, two, swapped)
    scal = jnp.stack([jnp.exp(log_scale), bias])
    return pl.pallas_call(
        tail_kernel,
        out_shape=jax.ShapeDtypeStruct((rows, width), jnp.bfloat16),
        in_specs=[smem, vmem, vmem] + [anyw] * 4,
        out_specs=vmem,
        scratch_shapes=[
            pltpu.VMEM((width, width), jnp.bfloat16),
            pltpu.VMEM((rows, width), jnp.float32),
            pltpu.SemaphoreType.DMA((4,)),
        ],
        compiler_params=pltpu.CompilerParams(vmem_limit_bytes=24 * 1024 * 1024),
        cost_estimate=pl.CostEstimate(
            flops=2 * 2 * rows * width * (width + 4 * rows),
            bytes_accessed=8 * 1024 * 1024,
            transcendentals=4 * rows * rows,
        ),
    )(scal, unit, text_feat, col, xcol, ocol, mcol)


def solution(mesh):
    placed = (P(AXES, None), P(AXES, None), P("dev", None), P(), P())
    return jax.shard_map(
        body, mesh=mesh, in_specs=placed, out_specs=P(AXES, None), check_vma=False
    )
```

```python
import jax
import jax.numpy as jnp
from jax import lax
from jax.experimental import pallas as pl
from jax.experimental.pallas import tpu as pltpu
from jax.sharding import PartitionSpec as P

norm_eps = 1e-06
AXES = ("island", "dev")
NX, NY, NZH = 4, 8, 2


def coords(i, n_dev):
    isl, dev = divmod(i, n_dev)
    return isl, dev // (NY * NZH), dev // NZH % NY, dev % NZH


def moved(value, to):
    n_isl, n_dev = lax.axis_size("island"), lax.axis_size("dev")
    pairs = []
    for i in range(n_isl * n_dev):
        target = to(*coords(i, n_dev))
        if target is not None:
            isl, x, y, zh = target
            pairs.append(
                (i, (isl % n_isl) * n_dev + ((x % NX) * NY + y % NY) * NZH + zh % NZH)
            )
    return lax.ppermute(value, AXES, pairs)


def place():
    isl = lax.axis_index("island").astype(jnp.int32)
    dev = lax.axis_index("dev").astype(jnp.int32)
    return dev >> 4, (dev >> 1) & 7, dev & 1, isl & 1, isl


def ordered(y, c, mine, other, out, at):
    for half in range(2):
        slabs = []
        for yy in range(half * 4, half * 4 + 4):
            j = (y - yy) & 7
            far = (j >= 4).astype(jnp.int32)
            pos = jnp.where(j < 4, j, 7 - j)
            slab = jnp.where(far == c, mine[pos], other[pos])
            slabs.append(slab.astype(jnp.float32))
        block = jnp.concatenate(slabs, axis=0).astype(jnp.bfloat16)
        out[pl.ds(at + half * 144, 144), :] = block


def column_kernel(mine, other, out):
    _, y, _, c, _ = place()
    ordered(y, c, mine, other, out, 0)


def column(mine, other):
    width = mine.shape[-1]
    return pl.pallas_call(
        column_kernel,
        out_shape=jax.ShapeDtypeStruct((NY * 36, width), jnp.bfloat16),
        cost_estimate=pl.CostEstimate(
            flops=NY * 36 * width, bytes_accessed=4 * NY * 36 * width, transcendentals=0
        ),
    )(mine, other)


def unit_kernel(im0, im1, wrap, im2, im3, out, raw, sems):
    rows = im0.shape[0]
    last = place()[4] == lax.axis_size("island") - 1
    copies = [
        pltpu.make_async_copy(src, raw.at[k], sems.at[k])
        for k, src in enumerate((im0, im1, im2, im3))
    ]
    for k in (0, 2, 3):
        copies[k].start()

    @pl.when(last)
    def _():
        pltpu.make_async_copy(wrap, raw.at[1], sems.at[1]).start()

    @pl.when(jnp.logical_not(last))
    def _():
        copies[1].start()

    for k in (0, 2, 3, 1):
        copies[k].wait()
        f = raw[k].astype(jnp.float32)
        s = lax.rsqrt(jnp.sum(f * f, axis=1, keepdims=True) + norm_eps)
        out[pl.ds(k * rows, rows), :] = (f * s).astype(jnp.bfloat16)


def tail_kernel(scal, unit, text, col, xcol, ocol, mcol, out_ref, full, hid, sems):
    x, _, _, c, _ = place()
    rows = out_ref.shape[0]
    step = jnp.where(c == 0, NX - 1, 1)
    wheres = (x, (x + step) & 3, (x + NX - step) & 3, (x + 2) & 3)
    copies = [
        pltpu.make_async_copy(src, full.at[pl.ds(pl.multiple_of(at * 288, 288), 288)], sems.at[k])
        for k, (src, at) in enumerate(zip((col, xcol, ocol, mcol), wheres))
    ]
    for copy in copies:
        copy.start()
    for copy in copies:
        copy.wait()
    hidden = jnp.dot(text[...], full[...], preferred_element_type=jnp.float32)
    inv = lax.rsqrt(jnp.sum(hidden * hidden, axis=1, keepdims=True) + norm_eps)
    hid[...] = hidden * inv
    text_b = hid[...].astype(jnp.bfloat16)
    scale, bias = scal[0], scal[1]
    scores = scale * lax.dot_general(
        text_b, unit[...], (((1,), (1,)), ((), ())), preferred_element_type=jnp.float32
    ) + bias
    r = lax.broadcasted_iota(jnp.int32, scores.shape, 0)
    s = lax.broadcasted_iota(jnp.int32, scores.shape, 1)
    probs = jax.nn.sigmoid(scores) - (r == s).astype(jnp.float32)
    grad = scale * jnp.dot(
        probs.astype(jnp.bfloat16), unit[...], preferred_element_type=jnp.float32
    )
    unit_txt = hid[...]
    radial = jnp.sum(unit_txt * grad, axis=1, keepdims=True)
    grad_hidden = ((grad - unit_txt * radial) * inv).astype(jnp.bfloat16)
    out_ref[...] = lax.dot_general(
        grad_hidden, full[...], (((1,), (1,)), ((), ())), preferred_element_type=jnp.float32
    ).astype(jnp.bfloat16)


def body(image_embed, text_feat, text_proj, log_scale, bias):
    rows, width = text_feat.shape
    x, y, zh, c, isl = place()
    n_isl = lax.axis_size("island")
    vmem = pl.BlockSpec(memory_space=pltpu.VMEM)
    smem = pl.BlockSpec(memory_space=pltpu.SMEM)
    anyw = pl.BlockSpec(memory_space=pl.ANY)

    far = moved(text_proj, lambda i, x, y, z: (i ^ 8, x, y - i % 2, 1 - z))
    near = moved(text_proj, lambda i, x, y, z: (i, x, y - 1, z) if i % 2 else None)
    base = jnp.where(c == 0, text_proj, near)
    pair = jnp.where(
        zh == 0, jnp.concatenate([base, far]), jnp.concatenate([far, base])
    )

    wrap2 = moved(image_embed, lambda i, x, y, z: (i - 2, x, y, z) if i < 2 else None)
    wrap3 = moved(image_embed, lambda i, x, y, z: (i - 3, x, y, z) if i == 2 else None)
    wrap2, wrap3 = lax.optimization_barrier((wrap2, wrap3))
    img = lax.optimization_barrier((image_embed, far))[0]
    near2 = moved(img, lambda i, x, y, z: (i - 2, x, y, z) if i >= 2 else None)
    two = jnp.where(isl >= n_isl - 2, wrap2, near2)

    got = [
        moved(pair, lambda i, x, y, z, k=k: (i, x, y + (-k if i % 2 else k), z))
        for k in (1, 2, 3)
    ]
    mine = jnp.stack([pair] + got)
    mine = lax.optimization_barrier((mine, wrap2))[0]
    mid = moved(mine, lambda i, x, y, z: (i, x + 2, y, z))
    other = moved(mine, lambda i, x, y, z: (i ^ 1, x, y, z))
    col = column(mine, other)
    xcol = moved(col, lambda i, x, y, z: (i, x + (-1 if i % 2 else 1), y, z))
    two_ = lax.optimization_barrier((two, col))[0]
    one = moved(
        jnp.where(c == 0, two_, image_embed),
        lambda i, x, y, z: (i - 1, x, y, z) if i > 0 else None,
    )
    swapped = moved(two_, lambda i, x, y, z: (i ^ 1, x, y, z))
    mid_ = mid
    omid = moved(mid_, lambda i, x, y, z: (i ^ 1, x, y, z))
    mcol = column(mid, omid)
    xcol_ = lax.optimization_barrier((xcol, mcol, one, swapped))[0]
    ocol = moved(xcol_, lambda i, x, y, z: (i ^ 1, x, y, z))

    unit = pl.pallas_call(
        unit_kernel,
        out_shape=jax.ShapeDtypeStruct((4 * rows, width), jnp.bfloat16),
        in_specs=[anyw] * 5,
        out_specs=vmem,
        scratch_shapes=[
            pltpu.VMEM((4, rows, width), jnp.bfloat16),
            pltpu.SemaphoreType.DMA((4,)),
        ],
        compiler_params=pltpu.CompilerParams(vmem_limit_bytes=16 * 1024 * 1024),
        cost_estimate=pl.CostEstimate(
            flops=12 * rows * width, bytes_accessed=16 * rows * width, transcendentals=4 * rows
        ),
    )(image_embed, one, wrap3, two, swapped)
    scal = jnp.stack([jnp.exp(log_scale), bias])
    return pl.pallas_call(
        tail_kernel,
        out_shape=jax.ShapeDtypeStruct((rows, width), jnp.bfloat16),
        in_specs=[smem, vmem, vmem] + [anyw] * 4,
        out_specs=vmem,
        scratch_shapes=[
            pltpu.VMEM((width, width), jnp.bfloat16),
            pltpu.VMEM((rows, width), jnp.float32),
            pltpu.SemaphoreType.DMA((4,)),
        ],
        compiler_params=pltpu.CompilerParams(vmem_limit_bytes=24 * 1024 * 1024),
        cost_estimate=pl.CostEstimate(
            flops=2 * 2 * rows * width * (width + 4 * rows),
            bytes_accessed=8 * 1024 * 1024,
            transcendentals=4 * rows * rows,
        ),
    )(scal, unit, text_feat, col, xcol, ocol, mcol)


def solution(mesh):
    placed = (P(AXES, None), P(AXES, None), P("dev", None), P(), P())
    return jax.shard_map(
        body, mesh=mesh, in_specs=placed, out_specs=P(AXES, None), check_vma=False
    )
```

```python
import jax
import jax.numpy as jnp
from jax import lax
from jax.experimental import pallas as pl
from jax.experimental.pallas import tpu as pltpu
from jax.sharding import PartitionSpec as P

norm_eps = 1e-06
AXES = ("island", "dev")
NX, NY, NZH = 4, 8, 2


def coords(i, n_dev):
    isl, dev = divmod(i, n_dev)
    return isl, dev // (NY * NZH), dev // NZH % NY, dev % NZH


def moved(value, to):
    n_isl, n_dev = lax.axis_size("island"), lax.axis_size("dev")
    pairs = []
    for i in range(n_isl * n_dev):
        target = to(*coords(i, n_dev))
        if target is not None:
            isl, x, y, zh = target
            pairs.append(
                (i, (isl % n_isl) * n_dev + ((x % NX) * NY + y % NY) * NZH + zh % NZH)
            )
    return lax.ppermute(value, AXES, pairs)


def place():
    isl = lax.axis_index("island").astype(jnp.int32)
    dev = lax.axis_index("dev").astype(jnp.int32)
    return dev >> 4, (dev >> 1) & 7, dev & 1, isl & 1, isl


def ordered(y, c, mine, other, out, at):
    for half in range(2):
        slabs = []
        for yy in range(half * 4, half * 4 + 4):
            j = (y - yy) & 7
            far = (j >= 4).astype(jnp.int32)
            pos = jnp.where(j < 4, j, 7 - j)
            slab = jnp.where(far == c, mine[pos], other[pos])
            slabs.append(slab.astype(jnp.float32))
        block = jnp.concatenate(slabs, axis=0).astype(jnp.bfloat16)
        out[pl.ds(at + half * 144, 144), :] = block


def column_kernel(mine, other, out):
    _, y, _, c, _ = place()
    ordered(y, c, mine, other, out, 0)


def column(mine, other):
    width = mine.shape[-1]
    return pl.pallas_call(
        column_kernel,
        out_shape=jax.ShapeDtypeStruct((NY * 36, width), jnp.bfloat16),
        cost_estimate=pl.CostEstimate(
            flops=NY * 36 * width, bytes_accessed=4 * NY * 36 * width, transcendentals=0
        ),
    )(mine, other)


def unit_kernel(im0, im1, wrap, im2, im3, out, raw, sems):
    rows = im0.shape[0]
    last = place()[4] == lax.axis_size("island") - 1
    copies = [
        pltpu.make_async_copy(src, raw.at[k], sems.at[k])
        for k, src in enumerate((im0, im1, im2, im3))
    ]
    for k in (0, 2, 3):
        copies[k].start()

    @pl.when(last)
    def _():
        pltpu.make_async_copy(wrap, raw.at[1], sems.at[1]).start()

    @pl.when(jnp.logical_not(last))
    def _():
        copies[1].start()

    for k in (0, 2, 3, 1):
        copies[k].wait()
        f = raw[k].astype(jnp.float32)
        s = lax.rsqrt(jnp.sum(f * f, axis=1, keepdims=True) + norm_eps)
        out[pl.ds(k * rows, rows), :] = (f * s).astype(jnp.bfloat16)


def tail_kernel(scal, unit, text, col, xcol, ocol, mcol, out_ref, full, hid, sems):
    x, _, _, c, _ = place()
    rows = out_ref.shape[0]
    step = jnp.where(c == 0, NX - 1, 1)
    wheres = (x, (x + step) & 3, (x + NX - step) & 3, (x + 2) & 3)
    copies = [
        pltpu.make_async_copy(src, full.at[pl.ds(pl.multiple_of(at * 288, 288), 288)], sems.at[k])
        for k, (src, at) in enumerate(zip((col, xcol, ocol, mcol), wheres))
    ]
    for copy in copies:
        copy.start()
    for copy in copies:
        copy.wait()
    hidden = jnp.dot(text[...], full[...], preferred_element_type=jnp.float32)
    inv = lax.rsqrt(jnp.sum(hidden * hidden, axis=1, keepdims=True) + norm_eps)
    hid[...] = hidden * inv
    text_b = hid[...].astype(jnp.bfloat16)
    scale, bias = scal[0], scal[1]
    scores = scale * lax.dot_general(
        text_b, unit[...], (((1,), (1,)), ((), ())), preferred_element_type=jnp.float32
    ) + bias
    r = lax.broadcasted_iota(jnp.int32, scores.shape, 0)
    s = lax.broadcasted_iota(jnp.int32, scores.shape, 1)
    probs = jax.nn.sigmoid(scores) - (r == s).astype(jnp.float32)
    grad = scale * jnp.dot(
        probs.astype(jnp.bfloat16), unit[...], preferred_element_type=jnp.float32
    )
    unit_txt = hid[...]
    radial = jnp.sum(unit_txt * grad, axis=1, keepdims=True)
    grad_hidden = ((grad - unit_txt * radial) * inv).astype(jnp.bfloat16)
    out_ref[...] = lax.dot_general(
        grad_hidden, full[...], (((1,), (1,)), ((), ())), preferred_element_type=jnp.float32
    ).astype(jnp.bfloat16)


def body(image_embed, text_feat, text_proj, log_scale, bias):
    rows, width = text_feat.shape
    x, y, zh, c, isl = place()
    n_isl = lax.axis_size("island")
    vmem = pl.BlockSpec(memory_space=pltpu.VMEM)
    smem = pl.BlockSpec(memory_space=pltpu.SMEM)
    anyw = pl.BlockSpec(memory_space=pl.ANY)

    far = moved(text_proj, lambda i, x, y, z: (i ^ 8, x, y - i % 2, 1 - z))
    near = moved(text_proj, lambda i, x, y, z: (i, x, y - 1, z) if i % 2 else None)
    base = jnp.where(c == 0, text_proj, near)
    pair = jnp.where(
        zh == 0, jnp.concatenate([base, far]), jnp.concatenate([far, base])
    )

    wrap2 = moved(image_embed, lambda i, x, y, z: (i - 2, x, y, z) if i < 2 else None)
    wrap3 = moved(image_embed, lambda i, x, y, z: (i - 3, x, y, z) if i == 2 else None)
    img = lax.optimization_barrier((image_embed, far))[0]
    near2 = moved(img, lambda i, x, y, z: (i - 2, x, y, z) if i >= 2 else None)
    two = jnp.where(isl >= n_isl - 2, wrap2, near2)

    got = [
        moved(pair, lambda i, x, y, z, k=k: (i, x, y + (-k if i % 2 else k), z))
        for k in (1, 2, 3)
    ]
    mine = jnp.stack([pair] + got)
    mine = lax.optimization_barrier((mine, wrap2))[0]
    mid = moved(mine, lambda i, x, y, z: (i, x + 2, y, z))
    other = moved(mine, lambda i, x, y, z: (i ^ 1, x, y, z))
    other = lax.optimization_barrier((other, wrap3))[0]
    col = column(mine, other)
    xcol = moved(col, lambda i, x, y, z: (i, x + (-1 if i % 2 else 1), y, z))
    two_ = lax.optimization_barrier((two, col))[0]
    one = moved(
        jnp.where(c == 0, two_, image_embed),
        lambda i, x, y, z: (i - 1, x, y, z) if i > 0 else None,
    )
    swapped = moved(two_, lambda i, x, y, z: (i ^ 1, x, y, z))
    mid_ = mid
    omid = moved(mid_, lambda i, x, y, z: (i ^ 1, x, y, z))
    mcol = column(mid, omid)
    xcol_ = lax.optimization_barrier((xcol, mcol, one, swapped))[0]
    ocol = moved(xcol_, lambda i, x, y, z: (i ^ 1, x, y, z))

    unit = pl.pallas_call(
        unit_kernel,
        out_shape=jax.ShapeDtypeStruct((4 * rows, width), jnp.bfloat16),
        in_specs=[anyw] * 5,
        out_specs=vmem,
        scratch_shapes=[
            pltpu.VMEM((4, rows, width), jnp.bfloat16),
            pltpu.SemaphoreType.DMA((4,)),
        ],
        compiler_params=pltpu.CompilerParams(vmem_limit_bytes=16 * 1024 * 1024),
        cost_estimate=pl.CostEstimate(
            flops=12 * rows * width, bytes_accessed=16 * rows * width, transcendentals=4 * rows
        ),
    )(image_embed, one, wrap3, two, swapped)
    scal = jnp.stack([jnp.exp(log_scale), bias])
    return pl.pallas_call(
        tail_kernel,
        out_shape=jax.ShapeDtypeStruct((rows, width), jnp.bfloat16),
        in_specs=[smem, vmem, vmem] + [anyw] * 4,
        out_specs=vmem,
        scratch_shapes=[
            pltpu.VMEM((width, width), jnp.bfloat16),
            pltpu.VMEM((rows, width), jnp.float32),
            pltpu.SemaphoreType.DMA((4,)),
        ],
        compiler_params=pltpu.CompilerParams(vmem_limit_bytes=24 * 1024 * 1024),
        cost_estimate=pl.CostEstimate(
            flops=2 * 2 * rows * width * (width + 4 * rows),
            bytes_accessed=8 * 1024 * 1024,
            transcendentals=4 * rows * rows,
        ),
    )(scal, unit, text_feat, col, xcol, ocol, mcol)


def solution(mesh):
    placed = (P(AXES, None), P(AXES, None), P("dev", None), P(), P())
    return jax.shard_map(
        body, mesh=mesh, in_specs=placed, out_specs=P(AXES, None), check_vma=False
    )
```

```python
import jax
import jax.numpy as jnp
from jax import lax
from jax.experimental import pallas as pl
from jax.experimental.pallas import tpu as pltpu
from jax.sharding import PartitionSpec as P

norm_eps = 1e-06
AXES = ("island", "dev")
NX, NY, NZH = 4, 8, 2


def coords(i, n_dev):
    isl, dev = divmod(i, n_dev)
    return isl, dev // (NY * NZH), dev // NZH % NY, dev % NZH


def moved(value, to):
    n_isl, n_dev = lax.axis_size("island"), lax.axis_size("dev")
    pairs = []
    for i in range(n_isl * n_dev):
        target = to(*coords(i, n_dev))
        if target is not None:
            isl, x, y, zh = target
            pairs.append(
                (i, (isl % n_isl) * n_dev + ((x % NX) * NY + y % NY) * NZH + zh % NZH)
            )
    return lax.ppermute(value, AXES, pairs)


def place():
    isl = lax.axis_index("island").astype(jnp.int32)
    dev = lax.axis_index("dev").astype(jnp.int32)
    return dev >> 4, (dev >> 1) & 7, dev & 1, isl & 1, isl


def ordered(y, c, mine, other, out, at):
    for half in range(2):
        slabs = []
        for yy in range(half * 4, half * 4 + 4):
            j = (y - yy) & 7
            far = (j >= 4).astype(jnp.int32)
            pos = jnp.where(j < 4, j, 7 - j)
            slab = jnp.where(far == c, mine[pos], other[pos])
            slabs.append(slab.astype(jnp.float32))
        block = jnp.concatenate(slabs, axis=0).astype(jnp.bfloat16)
        out[pl.ds(at + half * 144, 144), :] = block


def column_kernel(mine, other, out):
    _, y, _, c, _ = place()
    ordered(y, c, mine, other, out, 0)


def column(mine, other):
    width = mine.shape[-1]
    return pl.pallas_call(
        column_kernel,
        out_shape=jax.ShapeDtypeStruct((NY * 36, width), jnp.bfloat16),
        cost_estimate=pl.CostEstimate(
            flops=NY * 36 * width, bytes_accessed=4 * NY * 36 * width, transcendentals=0
        ),
    )(mine, other)


def unit_kernel(im0, im1, wrap, im2, im3, out, raw, sems):
    rows = im0.shape[0]
    last = place()[4] == lax.axis_size("island") - 1
    copies = [
        pltpu.make_async_copy(src, raw.at[k], sems.at[k])
        for k, src in enumerate((im0, im1, im2, im3))
    ]
    for k in (0, 2, 3):
        copies[k].start()

    @pl.when(last)
    def _():
        pltpu.make_async_copy(wrap, raw.at[1], sems.at[1]).start()

    @pl.when(jnp.logical_not(last))
    def _():
        copies[1].start()

    for k in (0, 2, 3, 1):
        copies[k].wait()
        f = raw[k].astype(jnp.float32)
        s = lax.rsqrt(jnp.sum(f * f, axis=1, keepdims=True) + norm_eps)
        out[pl.ds(k * rows, rows), :] = (f * s).astype(jnp.bfloat16)


def tail_kernel(scal, unit, text, col, xcol, ocol, mcol, out_ref, full, hid, sems):
    x, _, _, c, _ = place()
    rows = out_ref.shape[0]
    step = jnp.where(c == 0, NX - 1, 1)
    wheres = (x, (x + step) & 3, (x + NX - step) & 3, (x + 2) & 3)
    copies = [
        pltpu.make_async_copy(src, full.at[pl.ds(pl.multiple_of(at * 288, 288), 288)], sems.at[k])
        for k, (src, at) in enumerate(zip((col, xcol, ocol, mcol), wheres))
    ]
    for copy in copies:
        copy.start()
    for copy in copies:
        copy.wait()
    hidden = jnp.dot(text[...], full[...], preferred_element_type=jnp.float32)
    inv = lax.rsqrt(jnp.sum(hidden * hidden, axis=1, keepdims=True) + norm_eps)
    hid[...] = hidden * inv
    text_b = hid[...].astype(jnp.bfloat16)
    scale, bias = scal[0], scal[1]
    scores = scale * lax.dot_general(
        text_b, unit[...], (((1,), (1,)), ((), ())), preferred_element_type=jnp.float32
    ) + bias
    r = lax.broadcasted_iota(jnp.int32, scores.shape, 0)
    s = lax.broadcasted_iota(jnp.int32, scores.shape, 1)
    probs = jax.nn.sigmoid(scores) - (r == s).astype(jnp.float32)
    grad = scale * jnp.dot(
        probs.astype(jnp.bfloat16), unit[...], preferred_element_type=jnp.float32
    )
    unit_txt = hid[...]
    radial = jnp.sum(unit_txt * grad, axis=1, keepdims=True)
    grad_hidden = ((grad - unit_txt * radial) * inv).astype(jnp.bfloat16)
    out_ref[...] = lax.dot_general(
        grad_hidden, full[...], (((1,), (1,)), ((), ())), preferred_element_type=jnp.float32
    ).astype(jnp.bfloat16)


def body(image_embed, text_feat, text_proj, log_scale, bias):
    rows, width = text_feat.shape
    x, y, zh, c, isl = place()
    n_isl = lax.axis_size("island")
    vmem = pl.BlockSpec(memory_space=pltpu.VMEM)
    smem = pl.BlockSpec(memory_space=pltpu.SMEM)
    anyw = pl.BlockSpec(memory_space=pl.ANY)

    far = moved(text_proj, lambda i, x, y, z: (i ^ 8, x, y - i % 2, 1 - z))
    near = moved(text_proj, lambda i, x, y, z: (i, x, y - 1, z) if i % 2 else None)
    base = jnp.where(c == 0, text_proj, near)
    pair = jnp.where(
        zh == 0, jnp.concatenate([base, far]), jnp.concatenate([far, base])
    )

    wrap2 = moved(image_embed, lambda i, x, y, z: (i - 2, x, y, z) if i < 2 else None)
    wrap3 = moved(image_embed, lambda i, x, y, z: (i - 3, x, y, z) if i == 2 else None)
    img = lax.optimization_barrier((image_embed, far))[0]
    near2 = moved(img, lambda i, x, y, z: (i - 2, x, y, z) if i >= 2 else None)
    two = jnp.where(isl >= n_isl - 2, wrap2, near2)

    got = [
        moved(pair, lambda i, x, y, z, k=k: (i, x, y + (-k if i % 2 else k), z))
        for k in (1, 2, 3)
    ]
    mine = jnp.stack([pair] + got)
    mine = lax.optimization_barrier((mine, wrap2))[0]
    mid = moved(mine, lambda i, x, y, z: (i, x + 2, y, z))
    other = moved(mine, lambda i, x, y, z: (i ^ 1, x, y, z))
    col = column(mine, other)
    xcol = moved(col, lambda i, x, y, z: (i, x + (-1 if i % 2 else 1), y, z))
    two_ = lax.optimization_barrier((two, col))[0]
    one = moved(
        jnp.where(c == 0, two_, image_embed),
        lambda i, x, y, z: (i - 1, x, y, z) if i > 0 else None,
    )
    swapped = moved(two_, lambda i, x, y, z: (i ^ 1, x, y, z))
    mid_ = mid
    omid = moved(mid_, lambda i, x, y, z: (i ^ 1, x, y, z))
    mcol = column(mid, omid)
    xcol_ = lax.optimization_barrier((xcol, mcol, one, swapped, wrap3))[0]
    ocol = moved(xcol_, lambda i, x, y, z: (i ^ 1, x, y, z))

    unit = pl.pallas_call(
        unit_kernel,
        out_shape=jax.ShapeDtypeStruct((4 * rows, width), jnp.bfloat16),
        in_specs=[anyw] * 5,
        out_specs=vmem,
        scratch_shapes=[
            pltpu.VMEM((4, rows, width), jnp.bfloat16),
            pltpu.SemaphoreType.DMA((4,)),
        ],
        compiler_params=pltpu.CompilerParams(vmem_limit_bytes=16 * 1024 * 1024),
        cost_estimate=pl.CostEstimate(
            flops=12 * rows * width, bytes_accessed=16 * rows * width, transcendentals=4 * rows
        ),
    )(image_embed, one, wrap3, two, swapped)
    scal = jnp.stack([jnp.exp(log_scale), bias])
    return pl.pallas_call(
        tail_kernel,
        out_shape=jax.ShapeDtypeStruct((rows, width), jnp.bfloat16),
        in_specs=[smem, vmem, vmem] + [anyw] * 4,
        out_specs=vmem,
        scratch_shapes=[
            pltpu.VMEM((width, width), jnp.bfloat16),
            pltpu.VMEM((rows, width), jnp.float32),
            pltpu.SemaphoreType.DMA((4,)),
        ],
        compiler_params=pltpu.CompilerParams(vmem_limit_bytes=24 * 1024 * 1024),
        cost_estimate=pl.CostEstimate(
            flops=2 * 2 * rows * width * (width + 4 * rows),
            bytes_accessed=8 * 1024 * 1024,
            transcendentals=4 * rows * rows,
        ),
    )(scal, unit, text_feat, col, xcol, ocol, mcol)


def solution(mesh):
    placed = (P(AXES, None), P(AXES, None), P("dev", None), P(), P())
    return jax.shard_map(
        body, mesh=mesh, in_specs=placed, out_specs=P(AXES, None), check_vma=False
    )
```
